32 devices in a mesh: group: 2 (over y), section: 2 (over core), expert: 8 (over z, x).
Axes of the slice: x: 2, y: 2, z: 4, core: 2. Of those that a mesh axis runs over, the one named last changes fastest.
Arguments:
- activations: bfloat16 [64, 6144], P(('group', 'expert')), parts along dimension 0, may hold values from -6 to 6
- routes: int32 [2, 64, 2], P('section', ('group', 'expert')), parts along dimension 1, may hold values from 0 to 7, as said below
- norm_gain: bfloat16 [2, 6144], P('section'), may hold values from 0.099609375 to 1.8984375
- router: bfloat16 [2, 6144, 8], P('section'), may hold values from -0.078125 to 0.078125
- w_gate: bfloat16 [2, 6144, 1024], P('section', None, 'expert'), may hold values from -0.078125 to 0.078125
- w_up: bfloat16 [2, 6144, 1024], P('section', None, 'expert'), may hold values from -0.078125 to 0.078125
- w_down: bfloat16 [2, 1024, 6144], P('section', 'expert'), may hold values from -0.1875 to 0.1875
Outputs:
- section_out: bfloat16 [2, 64, 6144], P('section', ('group', 'expert')), parts along dimension 1
The draws below stay inside these ranges and needn't reach their ends.
There are 2 independent parts, one for each index of `group`. The reference program is written for one: setup_inputs(seed, part) draws one part's arguments, and reference() takes and returns one part's arrays. A program takes and returns all parts, laid end to end along the dimension named above; an argument that names none is the same for every part. Nothing has to cross between parts.
Inputs may be any that keep to these rules, and one draw needn't show every extreme that they name: `routes`: each row names 2 different experts; within the rows of one device (aligned blocks of 4 rows) no expert is named by more than 2 rows, and in each layer expert 0 is named by exactly 2 rows of some device.
All inputs are finite; a program needn't handle non-finite values.
Results may differ from the reference program's by a relative error of at most 0.005.
Values may be sent and summed in bfloat16 or wider, within the bound.
A program may use at most 64 MiB of HBM per device.

```python
import jax
import jax.numpy as jnp
from jax import lax

D = 6144
EXPERTS = 8
TOP = 2
EF = 1
HID_DEV = 128
TOK_DEV = 4
CAP = 2
SECTIONS = 2
SHARDS = 8
FF = 1024
ROWS = 32


def route_block(key, zero_count):
    fill_key, row_key, flip_key = jax.random.split(key, 3)
    slot_count = TOP * TOK_DEV
    pool = jnp.arange((EXPERTS - 1) * CAP, dtype=jnp.int32) // CAP + 1
    pool = jax.random.permutation(fill_key, pool)
    others = pool[:slot_count]
    position = jnp.arange(slot_count, dtype=jnp.int32)
    shifted = jnp.take(others, jnp.clip(position - zero_count, 0, slot_count - 1))
    labels = jnp.where(position < zero_count, 0, shifted).astype(jnp.int32)
    labels = jnp.sort(labels)
    table = labels.reshape(TOP, TOK_DEV).T
    flips = jax.random.randint(flip_key, (TOK_DEV, 1), 0, 2)
    table = jnp.where(flips == 1, table[:, ::-1], table)
    order = jax.random.permutation(row_key, TOK_DEV)
    return table[order]


def draw_routes(key, part):
    key = jax.random.fold_in(key, 11)
    block_count = ROWS // TOK_DEV
    count_key, force_key, block_key = jax.random.split(key, 3)
    counts = jax.random.randint(count_key, (SECTIONS, block_count), 0, CAP + 1)
    forced = jax.random.randint(force_key, (SECTIONS, 1), 0, block_count)
    block_iota = lax.broadcasted_iota(jnp.int32, (SECTIONS, block_count), 1)
    counts = jnp.where(block_iota == forced, CAP, counts).astype(jnp.int32).reshape(SECTIONS * block_count)
    keys = jax.random.split(block_key, SECTIONS * block_count)
    tables = jax.vmap(route_block)(keys, counts)
    return tables.reshape(SECTIONS, ROWS, TOP).astype(jnp.int32)


def block_levels(rng, shape, cuts, least, top_value):
    factor_of, own = 1.0, jax.random.fold_in(rng, 6)
    for dim, shards_of in cuts:
        steps = jnp.exp(jax.random.uniform(jax.random.fold_in(own, dim), (shards_of,), jnp.float32, least / len(cuts), top_value / len(cuts)))
        factor_of = factor_of * jnp.repeat(steps, shape[dim] // shards_of).reshape([-1 if axis == dim else 1 for axis in range(len(shape))])
    return factor_of


def bell_draw(stream_key, extent, width, limit, shards=(), held_as=jnp.bfloat16):
    result = jax.random.normal(stream_key, extent, jnp.float32) * width
    if len(shards) > 0:
        result = block_levels(stream_key, extent, shards, -0.22, 0.18) * result
    return jnp.clip(result, min=-limit, max=limit).astype(held_as)


def setup_inputs(seed: int = 0, part: int = 0) -> dict:
    arg_keys = jax.random.split(jax.random.key(seed), 8)
    own_keys = jax.random.split(jax.random.fold_in(arg_keys[7], part), 8)
    return {
        "activations": bell_draw(own_keys[0], (ROWS, D), 1.0, 6.0, ((0, 8),)),
        "routes": draw_routes(jax.random.fold_in(jax.random.fold_in(arg_keys[7], part), 71), part),
        "norm_gain": jnp.clip(1.0 + 0.18 * jax.random.normal(arg_keys[2], (SECTIONS, D), jnp.float32), 0.099609375, 1.8984375).astype(jnp.bfloat16),
        "router": bell_draw(arg_keys[3], (SECTIONS, D, EXPERTS), D ** -0.5, 0.078125, ((0, 2),)),
        "w_gate": bell_draw(arg_keys[4], (SECTIONS, D, EF * FF), D ** -0.5, 0.078125, ((0, 2), (2, 8))),
        "w_up": bell_draw(arg_keys[5], (SECTIONS, D, EF * FF), D ** -0.5, 0.078125, ((0, 2), (2, 8))),
        "w_down": bell_draw(arg_keys[6], (SECTIONS, EF * FF, D), FF ** -0.5, 0.1875, ((0, 2), (1, 8))),
    }


EPSILON = 1e-05

def moe_layer(inputs, route_ids, gain_row, router_w, gate_all, up_all, down_all):
    widened = inputs.astype(jnp.float32)
    inv_rms = lax.rsqrt(lax.optimization_barrier(jnp.mean(widened * widened, axis=-1, keepdims=True)) + EPSILON)
    normed = (widened * inv_rms * gain_row.astype(jnp.float32)).astype(jnp.bfloat16)
    logits = jnp.dot(normed, router_w, preferred_element_type=jnp.float32)
    chosen = jnp.take_along_axis(logits, route_ids, axis=1)
    gate_probs = jax.nn.softmax(chosen, axis=-1)
    block_count = ROWS // TOK_DEV
    blocks = normed.astype(jnp.float32).reshape(block_count, TOK_DEV, D)
    slot_iota = lax.broadcasted_iota(jnp.int32, (1, 1, CAP), 2)
    expert_sum = jnp.zeros((ROWS, D), jnp.float32)
    for held_idx in range(EF):
        is_named = route_ids == held_idx
        weight = lax.optimization_barrier(jnp.sum(jnp.where(is_named, gate_probs, 0.0), axis=1))
        marks = jnp.any(is_named, axis=1).astype(jnp.int32).reshape(block_count, TOK_DEV)
        rank = jnp.cumsum(marks, axis=1, dtype=jnp.int32) - marks
        place = ((rank[:, :, None] == slot_iota) & (marks[:, :, None] == 1)).astype(jnp.float32)
        slot_rows = jnp.einsum('brc,brd->bcd', place, blocks).astype(jnp.bfloat16).reshape(block_count * CAP, D)
        gate_pre = jnp.dot(slot_rows, gate_all[:, held_idx * FF:(held_idx + 1) * FF], preferred_element_type=jnp.float32)
        up_pre = jnp.dot(slot_rows, up_all[:, held_idx * FF:(held_idx + 1) * FF], preferred_element_type=jnp.float32)
        hidden = (jax.nn.silu(gate_pre) * up_pre).astype(jnp.bfloat16)
        down_rows = down_all[held_idx * FF:(held_idx + 1) * FF]

        def add_shard(running, shard_idx):
            offset = shard_idx * HID_DEV
            hid_block = lax.dynamic_slice_in_dim(hidden, offset, HID_DEV, 1)
            down_block = lax.dynamic_slice_in_dim(down_rows, offset, HID_DEV, 0)
            shard_term = jnp.dot(hid_block, down_block, preferred_element_type=jnp.float32).astype(jnp.bfloat16)
            shard_term = lax.optimization_barrier(shard_term)
            return (running + shard_term.astype(jnp.float32), None)
        expert_out, _ = lax.scan(add_shard, jnp.zeros((block_count * CAP, D), jnp.float32), jnp.arange(SHARDS, dtype=jnp.int32))
        back = jnp.einsum('brc,bcd->brd', place, expert_out.reshape(block_count, CAP, D)).reshape(ROWS, D)
        expert_sum = expert_sum + weight[:, None] * back
    return (widened + expert_sum).astype(jnp.bfloat16)

def reference(activations, routes, norm_gain, router, w_gate, w_up, w_down):
    current = activations
    outputs = []
    for layer_idx in range(SECTIONS):
        current = moe_layer(current, routes[layer_idx], norm_gain[layer_idx], router[layer_idx], w_gate[layer_idx], w_up[layer_idx], w_down[layer_idx])
        outputs.append(current)
    return jnp.stack(outputs)
```

```python
import functools

import jax
import jax.numpy as jnp
from jax import lax
from jax.experimental import pallas as pl
from jax.experimental.pallas import tpu as pltpu
from jax.sharding import PartitionSpec as P

EPSILON = 1e-05
CAP = 2
CHUNKS = 4


def far_first(n):
    return sorted(range(1, n), key=lambda k: (abs(k - n // 2), k))


def for_peers(n, me, body):
    if n <= 8:
        for k in far_first(n):
            body(lax.rem(me + k, n))
    else:
        def step(k, carry):
            body(lax.rem(me + k, n))
            return carry
        lax.fori_loop(1, n, step, 0)


def column(row):
    r = row.shape[1]
    eye = lax.broadcasted_iota(jnp.int32, (r, r), 0) == lax.broadcasted_iota(jnp.int32, (r, r), 1)
    return jnp.sum(jnp.where(eye, jnp.broadcast_to(row, (r, r)), 0.0), axis=1, keepdims=True)


def kernel(
    n, chunks,
    x_h, routes_ref, gain_h, router_h, wg_h, wu_h, wd_h,
    o_ref,
    x_v, gain_v, router_v, wgu_v, wd_v, normed_v, slot, gbuf, sbuf, rbuf, cw_v, cw_in, x1_v,
    lsem, wsem, gs_sem, gr_sem, ps_sem, pr_sem, msem,
):
    group = lax.axis_index("group")
    section = lax.axis_index("section")
    me = lax.axis_index("expert")
    rows, width = x_h.shape
    dk = width // chunks
    hid = wd_h.shape[1]

    small = [
        pltpu.make_async_copy(x_h, x_v, lsem.at[0]),
        pltpu.make_async_copy(gain_h, gain_v, lsem.at[1]),
        pltpu.make_async_copy(router_h, router_v, lsem.at[2]),
    ]
    for copy in small:
        copy.start()

    barrier = pltpu.get_barrier_semaphore()

    def greet(sec, peer):
        pl.semaphore_signal(
            barrier, inc=1, device_id=(group, sec, peer), device_id_type=pl.DeviceIdType.MESH
        )

    greet(1 - section, me)
    for_peers(n, me, lambda peer: greet(section, peer))

    @pl.when(section == 1)
    def _():
        for_peers(n, me, lambda peer: greet(0, peer))

    weights = []
    for c in range(chunks):
        part = pl.ds(c * dk, dk)
        weights.append([
            pltpu.make_async_copy(wg_h.at[0, part, :], wgu_v.at[part, pl.ds(0, hid)], wsem.at[0, c]),
            pltpu.make_async_copy(wu_h.at[0, part, :], wgu_v.at[part, pl.ds(hid, hid)], wsem.at[1, c]),
        ])
    down_copy = pltpu.make_async_copy(wd_h.at[0], wd_v, wsem.at[2, 0])
    for pair in weights:
        for copy in pair:
            copy.start()
    down_copy.start()

    def remote(src, dst, send_sem, recv_sem, sec, peer):
        return pltpu.make_async_remote_copy(
            src_ref=src, dst_ref=dst, send_sem=send_sem, recv_sem=recv_sem,
            device_id=(group, sec, peer), device_id_type=pl.DeviceIdType.MESH,
        )

    def wait_bytes(ref, sem):
        pltpu.make_async_copy(ref, ref, sem).wait()

    small[0].wait()
    small[1].wait()

    @pl.when(section == 0)
    def _():
        pl.semaphore_wait(barrier, 2 * n - 1)

    @pl.when(section == 1)
    def _():
        pl.semaphore_wait(barrier, n)

    first = column(routes_ref[0:1, :].astype(jnp.float32))
    second = column(routes_ref[1:2, :].astype(jnp.float32))
    marks = jnp.where((first == 0.0) | (second == 0.0), 1.0, 0.0)
    row_iota = lax.broadcasted_iota(jnp.int32, (rows, 1), 0)
    rank = jnp.zeros((rows, 1), jnp.float32)
    for q in range(rows - 1):
        rank += jnp.where(row_iota > q, jnp.broadcast_to(marks[q:q + 1, :], (rows, 1)), 0.0)
    places = [jnp.where(rank == float(c), marks, 0.0) for c in range(CAP)]

    def send_rows(src_ref):
        wide = src_ref[...].astype(jnp.float32)
        inv_rms = lax.rsqrt(jnp.mean(wide * wide, axis=-1, keepdims=True) + EPSILON)
        for c in range(chunks):
            part = pl.ds(c * dk, dk)
            normed = src_ref[:, part].astype(jnp.float32) * inv_rms * gain_v[:, part].astype(jnp.float32)
            normed = normed.astype(jnp.bfloat16)
            normed_v[:, part] = normed
            normed = normed.astype(jnp.float32)
            picked = [jnp.sum(normed * place, axis=0, keepdims=True) for place in places]
            block = jnp.concatenate(picked, axis=0).astype(jnp.bfloat16)
            slot[c] = block
            gbuf[c, me] = block
            for_peers(n, me, lambda peer: remote(
                slot.at[c], gbuf.at[c, me], gs_sem.at[c], gr_sem.at[c], section, peer).start())

    def combine_weights():
        logits = lax.dot_general(
            normed_v[...], router_v[...], (((1,), (1,)), ((), ())),
            preferred_element_type=jnp.float32,
        )
        ids = lax.broadcasted_iota(jnp.int32, logits.shape, 1).astype(jnp.float32)
        one = jnp.sum(jnp.where(ids == first, logits, 0.0), axis=1, keepdims=True)
        two = jnp.sum(jnp.where(ids == second, logits, 0.0), axis=1, keepdims=True)
        top = jnp.maximum(one, two)
        e_one, e_two = jnp.exp(one - top), jnp.exp(two - top)
        total = e_one + e_two
        weight = jnp.where(first == 0.0, e_one / total, 0.0) + jnp.where(second == 0.0, e_two / total, 0.0)
        lane = lax.broadcasted_iota(jnp.int32, (rows, 128), 1)
        packed = jnp.where(lane == 0, places[0] * weight, jnp.where(lane == 1, places[1] * weight, 0.0))
        cw_v[...] = packed

    def expert(layer, own):
        acc = jnp.zeros((CAP * n, 2 * hid), jnp.float32)
        for c in range(chunks):
            for copy in weights[c]:
                copy.wait()
            wait_bytes(gbuf.at[c, pl.ds(0, n - 1)], gr_sem.at[c])
            lhs = gbuf[c].astype(jnp.float32).reshape(CAP * n, dk).astype(jnp.bfloat16)
            acc += jnp.dot(lhs, wgu_v[pl.ds(c * dk, dk), :], preferred_element_type=jnp.float32)
        gate, up = acc[:, :hid], acc[:, hid:]
        hidden = (gate / (1.0 + jnp.exp(-gate)) * up).astype(jnp.bfloat16)
        down_copy.wait()
        for c in range(chunks):
            part = jnp.dot(hidden, wd_v[:, pl.ds(c * dk, dk)], preferred_element_type=jnp.float32)
            sbuf[c] = part.reshape(n, CAP, dk).astype(jnp.bfloat16)

            def send(peer):
                remote(
                    sbuf.at[c, peer], rbuf.at[c, me], ps_sem.at[c], pr_sem.at[c], 1, peer
                ).start()

            for_peers(n, me, send)
            if own:
                rbuf[c, me] = sbuf[c, me]
            else:
                send(me)

    def combine(c, count, base, cw):
        wait_bytes(rbuf.at[c, pl.ds(0, count)], pr_sem.at[c])
        summed = jnp.sum(rbuf[c].astype(jnp.float32), axis=0)
        total = base + cw[:, 0:1] * summed[0:1, :] + cw[:, 1:2] * summed[1:2, :]
        return total.astype(jnp.bfloat16)

    def drain_rows():
        for c in range(chunks):
            wait_bytes(gbuf.at[c, pl.ds(0, n - 1)], gs_sem.at[c])

    def drain_partials(count):
        for c in range(chunks):
            wait_bytes(sbuf.at[c, pl.ds(0, count)], ps_sem.at[c])

    @pl.when(section == 0)
    def _():
        send_rows(x_v)
        small[2].wait()
        combine_weights()
        weigh = remote(cw_v, cw_in, msem.at[0], msem.at[1], 1, me)
        weigh.start()
        expert(0, False)
        drain_rows()
        weigh.wait_send()
        drain_partials(n)
        wait_bytes(o_ref.at[0], msem.at[3])

    @pl.when(section == 1)
    def _():
        wait_bytes(cw_in, msem.at[1])
        cw0 = cw_in[...]
        for c in range(chunks):
            part = pl.ds(c * dk, dk)
            x1_v[:, part] = combine(c, n, x_v[:, part].astype(jnp.float32), cw0)
        send_rows(x1_v)
        back = remote(x1_v, o_ref.at[0], msem.at[2], msem.at[3], 0, me)
        back.start()
        small[2].wait()
        combine_weights()
        expert(1, True)
        cw1 = cw_v[...]
        for c in range(chunks):
            part = pl.ds(c * dk, dk)
            o_ref[0, :, part] = combine(c, n - 1, x1_v[:, part].astype(jnp.float32), cw1)
        drain_rows()
        back.wait_send()
        drain_partials(n - 1)


def per_device(activations, routes, norm_gain, router, w_gate, w_up, w_down):
    rows, width = activations.shape
    n = lax.axis_size("expert")
    hid = w_down.shape[1]
    chunks = CHUNKS
    dk = width // chunks
    bf16, f32 = jnp.bfloat16, jnp.float32
    dma = pltpu.SemaphoreType.DMA
    anywhere = pl.BlockSpec(memory_space=pl.ANY)
    vmem = pl.BlockSpec(memory_space=pltpu.VMEM)
    return pl.pallas_call(
        functools.partial(kernel, n, chunks),
        out_shape=jax.ShapeDtypeStruct((1, rows, width), bf16),
        in_specs=[anywhere, vmem, anywhere, anywhere, anywhere, anywhere, anywhere],
        out_specs=vmem,
        scratch_shapes=[
            pltpu.VMEM((rows, width), bf16),
            pltpu.VMEM((1, width), bf16),
            pltpu.VMEM((router.shape[2], width), bf16),
            pltpu.VMEM((width, 2 * hid), bf16),
            pltpu.VMEM((hid, width), bf16),
            pltpu.VMEM((rows, width), bf16),
            pltpu.VMEM((chunks, CAP, dk), bf16),
            pltpu.VMEM((chunks, n, CAP, dk), bf16),
            pltpu.VMEM((chunks, n, CAP, dk), bf16),
            pltpu.VMEM((chunks, n, CAP, dk), bf16),
            pltpu.VMEM((rows, 128), f32),
            pltpu.VMEM((rows, 128), f32),
            pltpu.VMEM((rows, width), bf16),
            dma((3,)),
            dma((3, chunks)),
            dma((chunks,)),
            dma((chunks,)),
            dma((chunks,)),
            dma((chunks,)),
            dma((4,)),
        ],
        compiler_params=pltpu.CompilerParams(
            collective_id=0, has_side_effects=True, vmem_limit_bytes=48 * 2**20
        ),
    )(activations, routes[0].T, norm_gain, router[0].T, w_gate, w_up, w_down)


def solution(mesh):
    in_specs = (
        P(("group", "expert"), None),
        P("section", ("group", "expert"), None),
        P("section", None),
        P("section", None, None),
        P("section", None, "expert"),
        P("section", None, "expert"),
        P("section", "expert", None),
    )
    out_specs = P("section", ("group", "expert"), None)
    return jax.shard_map(
        per_device, mesh=mesh, in_specs=in_specs, out_specs=out_specs, check_vma=False
    )
```

```python
import functools

import jax
import jax.numpy as jnp
from jax import lax
from jax.experimental import pallas as pl
from jax.experimental.pallas import tpu as pltpu
from jax.sharding import PartitionSpec as P

EPSILON = 1e-05
CAP = 2
CHUNKS = 4


def far_first(n):
    return sorted(range(1, n), key=lambda k: (abs(k - n // 2), k))


def for_peers(n, me, body):
    if n <= 8:
        for k in far_first(n):
            body(lax.rem(me + k, n))
    else:
        def step(k, carry):
            body(lax.rem(me + k, n))
            return carry
        lax.fori_loop(1, n, step, 0)


def column(row):
    r = row.shape[1]
    eye = lax.broadcasted_iota(jnp.int32, (r, r), 0) == lax.broadcasted_iota(jnp.int32, (r, r), 1)
    return jnp.sum(jnp.where(eye, jnp.broadcast_to(row, (r, r)), 0.0), axis=1, keepdims=True)


def kernel(
    n, chunks,
    x_h, routes_h, gain_h, router_h, wg_h, wu_h, wd_h,
    o_ref,
    x_v, routes_ref, gain_v, router_v, wgu_v, wd_v, normed_v, slot, gbuf, sbuf, rbuf, cw_v, cw_in, x1_v,
    lsem, wsem, gs_sem, gr_sem, ps_sem, pr_sem, msem,
):
    group = lax.axis_index("group")
    section = lax.axis_index("section")
    me = lax.axis_index("expert")
    rows, width = x_h.shape
    dk = width // chunks
    hid = wd_h.shape[1]

    small = [
        pltpu.make_async_copy(x_h, x_v, lsem.at[0]),
        pltpu.make_async_copy(gain_h, gain_v, lsem.at[1]),
        pltpu.make_async_copy(router_h, router_v, lsem.at[2]),
        pltpu.make_async_copy(routes_h, routes_ref, lsem.at[3]),
    ]
    for copy in small:
        copy.start()

    barrier = pltpu.get_barrier_semaphore()

    def greet(sec, peer):
        pl.semaphore_signal(
            barrier, inc=1, device_id=(group, sec, peer), device_id_type=pl.DeviceIdType.MESH
        )

    greet(1 - section, me)
    for_peers(n, me, lambda peer: greet(section, peer))

    @pl.when(section == 1)
    def _():
        for_peers(n, me, lambda peer: greet(0, peer))

    weights = []
    for c in range(chunks):
        part = pl.ds(c * dk, dk)
        weights.append([
            pltpu.make_async_copy(wg_h.at[0, part, :], wgu_v.at[part, pl.ds(0, hid)], wsem.at[0, c]),
            pltpu.make_async_copy(wu_h.at[0, part, :], wgu_v.at[part, pl.ds(hid, hid)], wsem.at[1, c]),
        ])
    down_copy = pltpu.make_async_copy(wd_h.at[0], wd_v, wsem.at[2, 0])
    for pair in weights:
        for copy in pair:
            copy.start()
    down_copy.start()

    def remote(src, dst, send_sem, recv_sem, sec, peer):
        return pltpu.make_async_remote_copy(
            src_ref=src, dst_ref=dst, send_sem=send_sem, recv_sem=recv_sem,
            device_id=(group, sec, peer), device_id_type=pl.DeviceIdType.MESH,
        )

    def wait_bytes(ref, sem):
        pltpu.make_async_copy(ref, ref, sem).wait()

    small[0].wait()
    small[1].wait()

    @pl.when(section == 0)
    def _():
        pl.semaphore_wait(barrier, 2 * n - 1)

    @pl.when(section == 1)
    def _():
        pl.semaphore_wait(barrier, n)

    small[3].wait()
    first = column(routes_ref[0:1, :].astype(jnp.float32))
    second = column(routes_ref[1:2, :].astype(jnp.float32))
    marks = jnp.where((first == 0.0) | (second == 0.0), 1.0, 0.0)
    row_iota = lax.broadcasted_iota(jnp.int32, (rows, 1), 0)
    rank = jnp.zeros((rows, 1), jnp.float32)
    for q in range(rows - 1):
        rank += jnp.where(row_iota > q, jnp.broadcast_to(marks[q:q + 1, :], (rows, 1)), 0.0)
    places = [jnp.where(rank == float(c), marks, 0.0) for c in range(CAP)]

    def send_rows(src_ref):
        wide = src_ref[...].astype(jnp.float32)
        inv_rms = lax.rsqrt(jnp.mean(wide * wide, axis=-1, keepdims=True) + EPSILON)
        for c in range(chunks):
            part = pl.ds(c * dk, dk)
            normed = src_ref[:, part].astype(jnp.float32) * inv_rms * gain_v[:, part].astype(jnp.float32)
            normed = normed.astype(jnp.bfloat16)
            normed_v[:, part] = normed
            normed = normed.astype(jnp.float32)
            picked = [jnp.sum(normed * place, axis=0, keepdims=True) for place in places]
            block = jnp.concatenate(picked, axis=0).astype(jnp.bfloat16)
            slot[c] = block
            gbuf[c, me] = block
            for_peers(n, me, lambda peer: remote(
                slot.at[c], gbuf.at[c, me], gs_sem.at[c], gr_sem.at[c], section, peer).start())

    def combine_weights():
        logits = lax.dot_general(
            normed_v[...], router_v[...], (((1,), (1,)), ((), ())),
            preferred_element_type=jnp.float32,
        )
        ids = lax.broadcasted_iota(jnp.int32, logits.shape, 1).astype(jnp.float32)
        one = jnp.sum(jnp.where(ids == first, logits, 0.0), axis=1, keepdims=True)
        two = jnp.sum(jnp.where(ids == second, logits, 0.0), axis=1, keepdims=True)
        top = jnp.maximum(one, two)
        e_one, e_two = jnp.exp(one - top), jnp.exp(two - top)
        total = e_one + e_two
        weight = jnp.where(first == 0.0, e_one / total, 0.0) + jnp.where(second == 0.0, e_two / total, 0.0)
        lane = lax.broadcasted_iota(jnp.int32, (rows, 128), 1)
        packed = jnp.where(lane == 0, places[0] * weight, jnp.where(lane == 1, places[1] * weight, 0.0))
        cw_v[...] = packed

    def expert(layer, own):
        acc = jnp.zeros((CAP * n, 2 * hid), jnp.float32)
        for c in range(chunks):
            for copy in weights[c]:
                copy.wait()
            wait_bytes(gbuf.at[c, pl.ds(0, n - 1)], gr_sem.at[c])
            lhs = gbuf[c].astype(jnp.float32).reshape(CAP * n, dk).astype(jnp.bfloat16)
            acc += jnp.dot(lhs, wgu_v[pl.ds(c * dk, dk), :], preferred_element_type=jnp.float32)
        gate, up = acc[:, :hid], acc[:, hid:]
        hidden = (gate / (1.0 + jnp.exp(-gate)) * up).astype(jnp.bfloat16)
        down_copy.wait()
        for c in range(chunks):
            part = jnp.dot(hidden, wd_v[:, pl.ds(c * dk, dk)], preferred_element_type=jnp.float32)
            sbuf[c] = part.reshape(n, CAP, dk).astype(jnp.bfloat16)

            def send(peer):
                remote(
                    sbuf.at[c, peer], rbuf.at[c, me], ps_sem.at[c], pr_sem.at[c], 1, peer
                ).start()

            for_peers(n, me, send)
            if own:
                rbuf[c, me] = sbuf[c, me]
            else:
                send(me)

    def combine(c, count, base, cw):
        wait_bytes(rbuf.at[c, pl.ds(0, count)], pr_sem.at[c])
        summed = jnp.sum(rbuf[c].astype(jnp.float32), axis=0)
        total = base + cw[:, 0:1] * summed[0:1, :] + cw[:, 1:2] * summed[1:2, :]
        return total.astype(jnp.bfloat16)

    def drain_rows():
        for c in range(chunks):
            wait_bytes(gbuf.at[c, pl.ds(0, n - 1)], gs_sem.at[c])

    def drain_partials(count):
        for c in range(chunks):
            wait_bytes(sbuf.at[c, pl.ds(0, count)], ps_sem.at[c])

    @pl.when(section == 0)
    def _():
        send_rows(x_v)
        small[2].wait()
        combine_weights()
        weigh = remote(cw_v, cw_in, msem.at[0], msem.at[1], 1, me)
        weigh.start()
        expert(0, False)
        drain_rows()
        weigh.wait_send()
        drain_partials(n)
        wait_bytes(o_ref.at[0], msem.at[3])

    @pl.when(section == 1)
    def _():
        wait_bytes(cw_in, msem.at[1])
        cw0 = cw_in[...]
        for c in range(chunks):
            part = pl.ds(c * dk, dk)
            x1_v[:, part] = combine(c, n, x_v[:, part].astype(jnp.float32), cw0)
        send_rows(x1_v)
        back = remote(x1_v, o_ref.at[0], msem.at[2], msem.at[3], 0, me)
        back.start()
        small[2].wait()
        combine_weights()
        expert(1, True)
        cw1 = cw_v[...]
        for c in range(chunks):
            part = pl.ds(c * dk, dk)
            o_ref[0, :, part] = combine(c, n - 1, x1_v[:, part].astype(jnp.float32), cw1)
        drain_rows()
        back.wait_send()
        drain_partials(n - 1)


def per_device(activations, routes, norm_gain, router, w_gate, w_up, w_down):
    rows, width = activations.shape
    n = lax.axis_size("expert")
    hid = w_down.shape[1]
    chunks = CHUNKS
    dk = width // chunks
    bf16, f32 = jnp.bfloat16, jnp.float32
    dma = pltpu.SemaphoreType.DMA
    hbm = pl.BlockSpec(memory_space=pltpu.HBM)
    vmem = pl.BlockSpec(memory_space=pltpu.VMEM)
    return pl.pallas_call(
        functools.partial(kernel, n, chunks),
        out_shape=pltpu.VMEM((1, rows, width), bf16),
        in_specs=[hbm] * 7,
        out_specs=vmem,
        scratch_shapes=[
            pltpu.VMEM((rows, width), bf16),
            pltpu.VMEM((routes.shape[2], rows), jnp.int32),
            pltpu.VMEM((1, width), bf16),
            pltpu.VMEM((router.shape[2], width), bf16),
            pltpu.VMEM((width, 2 * hid), bf16),
            pltpu.VMEM((hid, width), bf16),
            pltpu.VMEM((rows, width), bf16),
            pltpu.VMEM((chunks, CAP, dk), bf16),
            pltpu.VMEM((chunks, n, CAP, dk), bf16),
            pltpu.VMEM((chunks, n, CAP, dk), bf16),
            pltpu.VMEM((chunks, n, CAP, dk), bf16),
            pltpu.VMEM((rows, 128), f32),
            pltpu.VMEM((rows, 128), f32),
            pltpu.VMEM((rows, width), bf16),
            dma((4,)),
            dma((3, chunks)),
            dma((chunks,)),
            dma((chunks,)),
            dma((chunks,)),
            dma((chunks,)),
            dma((4,)),
        ],
        compiler_params=pltpu.CompilerParams(
            collective_id=0, has_side_effects=True, vmem_limit_bytes=48 * 2**20
        ),
    )(*[pltpu.with_memory_space_constraint(v, pltpu.HBM) for v in (activations, routes[0].T, norm_gain, router[0].T, w_gate, w_up, w_down)])


def solution(mesh):
    in_specs = (
        P(("group", "expert"), None),
        P("section", ("group", "expert"), None),
        P("section", None),
        P("section", None, None),
        P("section", None, "expert"),
        P("section", None, "expert"),
        P("section", "expert", None),
    )
    out_specs = P("section", ("group", "expert"), None)
    return jax.shard_map(
        per_device, mesh=mesh, in_specs=in_specs, out_specs=out_specs, check_vma=False
    )
```

```python
import functools

import jax
import jax.numpy as jnp
from jax import lax
from jax.experimental import pallas as pl
from jax.experimental.pallas import tpu as pltpu
from jax.sharding import PartitionSpec as P

EPSILON = 1e-05
CAP = 2
CHUNKS = 4


def partner(me, k):
    peer, bit = me, 1
    while bit <= k:
        if k & bit:
            peer = peer + bit * (1 - 2 * lax.rem(me // bit, 2))
        bit *= 2
    return peer


def for_peers(n, me, body):
    if n in (2, 4, 8):
        for k in range(n - 1, 0, -1):
            body(partner(me, k))
    else:
        def step(k, carry):
            body(lax.rem(me + k, n))
            return carry
        lax.fori_loop(1, n, step, 0)


def column(row):
    r = row.shape[1]
    eye = lax.broadcasted_iota(jnp.int32, (r, r), 0) == lax.broadcasted_iota(jnp.int32, (r, r), 1)
    return jnp.sum(jnp.where(eye, jnp.broadcast_to(row, (r, r)), 0.0), axis=1, keepdims=True)


def kernel(
    n, chunks,
    x_h, routes_h, gain_h, router_h, wg_h, wu_h, wd_h,
    o_ref,
    x_v, routes_ref, gain_v, router_v, wgu_v, wd_v, normed_v, slot, gbuf, sbuf, rbuf, cw_v, cw_in, x1_v,
    lsem, wsem, gs_sem, gr_sem, ps_sem, pr_sem, msem,
):
    group = lax.axis_index("group")
    section = lax.axis_index("section")
    me = lax.axis_index("expert")
    rows, width = x_h.shape
    dk = width // chunks
    hid = wd_h.shape[1]

    small = [
        pltpu.make_async_copy(x_h, x_v, lsem.at[0]),
        pltpu.make_async_copy(gain_h, gain_v, lsem.at[1]),
        pltpu.make_async_copy(router_h, router_v, lsem.at[2]),
        pltpu.make_async_copy(routes_h, routes_ref, lsem.at[3]),
    ]
    for copy in small:
        copy.start()

    barrier = pltpu.get_barrier_semaphore()

    def greet(sec, peer):
        pl.semaphore_signal(
            barrier, inc=1, device_id=(group, sec, peer), device_id_type=pl.DeviceIdType.MESH
        )

    greet(1 - section, me)
    for_peers(n, me, lambda peer: greet(section, peer))

    @pl.when(section == 1)
    def _():
        for_peers(n, me, lambda peer: greet(0, peer))

    weights = []
    for c in range(chunks):
        part = pl.ds(c * dk, dk)
        weights.append([
            pltpu.make_async_copy(wg_h.at[0, part, :], wgu_v.at[part, pl.ds(0, hid)], wsem.at[0, c]),
            pltpu.make_async_copy(wu_h.at[0, part, :], wgu_v.at[part, pl.ds(hid, hid)], wsem.at[1, c]),
        ])
    down_copy = pltpu.make_async_copy(wd_h.at[0], wd_v, wsem.at[2, 0])
    for pair in weights:
        for copy in pair:
            copy.start()
    down_copy.start()

    def remote(src, dst, send_sem, recv_sem, sec, peer):
        return pltpu.make_async_remote_copy(
            src_ref=src, dst_ref=dst, send_sem=send_sem, recv_sem=recv_sem,
            device_id=(group, sec, peer), device_id_type=pl.DeviceIdType.MESH,
        )

    def wait_bytes(ref, sem):
        pltpu.make_async_copy(ref, ref, sem).wait()

    small[0].wait()
    small[1].wait()

    @pl.when(section == 0)
    def _():
        pl.semaphore_wait(barrier, 2 * n - 1)

    @pl.when(section == 1)
    def _():
        pl.semaphore_wait(barrier, n)

    small[3].wait()
    first = column(routes_ref[0:1, :].astype(jnp.float32))
    second = column(routes_ref[1:2, :].astype(jnp.float32))
    marks = jnp.where((first == 0.0) | (second == 0.0), 1.0, 0.0)
    row_iota = lax.broadcasted_iota(jnp.int32, (rows, 1), 0)
    rank = jnp.zeros((rows, 1), jnp.float32)
    for q in range(rows - 1):
        rank += jnp.where(row_iota > q, jnp.broadcast_to(marks[q:q + 1, :], (rows, 1)), 0.0)
    places = [jnp.where(rank == float(c), marks, 0.0) for c in range(CAP)]

    def send_rows(src_ref):
        wide = src_ref[...].astype(jnp.float32)
        inv_rms = lax.rsqrt(jnp.mean(wide * wide, axis=-1, keepdims=True) + EPSILON)
        for c in range(chunks):
            part = pl.ds(c * dk, dk)
            normed = src_ref[:, part].astype(jnp.float32) * inv_rms * gain_v[:, part].astype(jnp.float32)
            normed = normed.astype(jnp.bfloat16)
            normed_v[:, part] = normed
            normed = normed.astype(jnp.float32)
            picked = [jnp.sum(normed * place, axis=0, keepdims=True) for place in places]
            block = jnp.concatenate(picked, axis=0).astype(jnp.bfloat16)
            slot[c] = block
            gbuf[c, me] = block
            for_peers(n, me, lambda peer: remote(
                slot.at[c], gbuf.at[c, me], gs_sem.at[c], gr_sem.at[c], section, peer).start())

    def combine_weights():
        logits = lax.dot_general(
            normed_v[...], router_v[...], (((1,), (1,)), ((), ())),
            preferred_element_type=jnp.float32,
        )
        ids = lax.broadcasted_iota(jnp.int32, logits.shape, 1).astype(jnp.float32)
        one = jnp.sum(jnp.where(ids == first, logits, 0.0), axis=1, keepdims=True)
        two = jnp.sum(jnp.where(ids == second, logits, 0.0), axis=1, keepdims=True)
        top = jnp.maximum(one, two)
        e_one, e_two = jnp.exp(one - top), jnp.exp(two - top)
        total = e_one + e_two
        weight = jnp.where(first == 0.0, e_one / total, 0.0) + jnp.where(second == 0.0, e_two / total, 0.0)
        lane = lax.broadcasted_iota(jnp.int32, (rows, 128), 1)
        packed = jnp.where(lane == 0, places[0] * weight, jnp.where(lane == 1, places[1] * weight, 0.0))
        cw_v[...] = packed

    def expert(layer, own):
        acc = jnp.zeros((CAP * n, 2 * hid), jnp.float32)
        for c in range(chunks):
            for copy in weights[c]:
                copy.wait()
            wait_bytes(gbuf.at[c, pl.ds(0, n - 1)], gr_sem.at[c])
            lhs = gbuf[c].astype(jnp.float32).reshape(CAP * n, dk).astype(jnp.bfloat16)
            acc += jnp.dot(lhs, wgu_v[pl.ds(c * dk, dk), :], preferred_element_type=jnp.float32)
        gate, up = acc[:, :hid], acc[:, hid:]
        hidden = (gate / (1.0 + jnp.exp(-gate)) * up).astype(jnp.bfloat16)
        down_copy.wait()
        for c in range(chunks):
            part = jnp.dot(hidden, wd_v[:, pl.ds(c * dk, dk)], preferred_element_type=jnp.float32)
            sbuf[c] = part.reshape(n, CAP, dk).astype(jnp.bfloat16)

            def send(peer):
                remote(
                    sbuf.at[c, peer], rbuf.at[c, me], ps_sem.at[c], pr_sem.at[c], 1, peer
                ).start()

            for_peers(n, me, send)
            if own:
                rbuf[c, me] = sbuf[c, me]
            else:
                send(me)

    def combine(c, count, base, cw):
        wait_bytes(rbuf.at[c, pl.ds(0, count)], pr_sem.at[c])
        summed = jnp.sum(rbuf[c].astype(jnp.float32), axis=0)
        total = base + cw[:, 0:1] * summed[0:1, :] + cw[:, 1:2] * summed[1:2, :]
        return total.astype(jnp.bfloat16)

    def drain_rows():
        for c in range(chunks):
            wait_bytes(gbuf.at[c, pl.ds(0, n - 1)], gs_sem.at[c])

    def drain_partials(count):
        for c in range(chunks):
            wait_bytes(sbuf.at[c, pl.ds(0, count)], ps_sem.at[c])

    @pl.when(section == 0)
    def _():
        send_rows(x_v)
        small[2].wait()
        combine_weights()
        weigh = remote(cw_v, cw_in, msem.at[0], msem.at[1], 1, me)
        weigh.start()
        expert(0, False)
        drain_rows()
        weigh.wait_send()
        drain_partials(n)
        wait_bytes(o_ref.at[0], msem.at[3])

    @pl.when(section == 1)
    def _():
        wait_bytes(cw_in, msem.at[1])
        cw0 = cw_in[...]
        for c in range(chunks):
            part = pl.ds(c * dk, dk)
            x1_v[:, part] = combine(c, n, x_v[:, part].astype(jnp.float32), cw0)
        send_rows(x1_v)
        back = remote(x1_v, o_ref.at[0], msem.at[2], msem.at[3], 0, me)
        back.start()
        small[2].wait()
        combine_weights()
        expert(1, True)
        cw1 = cw_v[...]
        for c in range(chunks):
            part = pl.ds(c * dk, dk)
            o_ref[0, :, part] = combine(c, n - 1, x1_v[:, part].astype(jnp.float32), cw1)
        drain_rows()
        back.wait_send()
        drain_partials(n - 1)


def per_device(activations, routes, norm_gain, router, w_gate, w_up, w_down):
    rows, width = activations.shape
    n = lax.axis_size("expert")
    hid = w_down.shape[1]
    chunks = CHUNKS
    dk = width // chunks
    bf16, f32 = jnp.bfloat16, jnp.float32
    dma = pltpu.SemaphoreType.DMA
    hbm = pl.BlockSpec(memory_space=pltpu.HBM)
    vmem = pl.BlockSpec(memory_space=pltpu.VMEM)
    return pl.pallas_call(
        functools.partial(kernel, n, chunks),
        out_shape=pltpu.VMEM((1, rows, width), bf16),
        in_specs=[hbm] * 7,
        out_specs=vmem,
        scratch_shapes=[
            pltpu.VMEM((rows, width), bf16),
            pltpu.VMEM((routes.shape[2], rows), jnp.int32),
            pltpu.VMEM((1, width), bf16),
            pltpu.VMEM((router.shape[2], width), bf16),
            pltpu.VMEM((width, 2 * hid), bf16),
            pltpu.VMEM((hid, width), bf16),
            pltpu.VMEM((rows, width), bf16),
            pltpu.VMEM((chunks, CAP, dk), bf16),
            pltpu.VMEM((chunks, n, CAP, dk), bf16),
            pltpu.VMEM((chunks, n, CAP, dk), bf16),
            pltpu.VMEM((chunks, n, CAP, dk), bf16),
            pltpu.VMEM((rows, 128), f32),
            pltpu.VMEM((rows, 128), f32),
            pltpu.VMEM((rows, width), bf16),
            dma((4,)),
            dma((3, chunks)),
            dma((chunks,)),
            dma((chunks,)),
            dma((chunks,)),
            dma((chunks,)),
            dma((4,)),
        ],
        compiler_params=pltpu.CompilerParams(
            collective_id=0, has_side_effects=True, vmem_limit_bytes=48 * 2**20
        ),
    )(*[pltpu.with_memory_space_constraint(v, pltpu.HBM) for v in (activations, routes[0].T, norm_gain, router[0].T, w_gate, w_up, w_down)])


def solution(mesh):
    in_specs = (
        P(("group", "expert"), None),
        P("section", ("group", "expert"), None),
        P("section", None),
        P("section", None, None),
        P("section", None, "expert"),
        P("section", None, "expert"),
        P("section", "expert", None),
    )
    out_specs = P("section", ("group", "expert"), None)
    return jax.shard_map(
        per_device, mesh=mesh, in_specs=in_specs, out_specs=out_specs, check_vma=False
    )
```
